32 devices in a mesh: grp: 2 (over x), sec: 16 (over z, y, core).
Axes of the slice: x: 2, y: 2, z: 4, core: 2. Of those that a mesh axis runs over, the one named last changes fastest.
Arguments:
- psi_init: float32 [32, 64, 128], P(('grp', 'sec')), parts along dimension 0, may hold values from -6 to 6
- precond: float32 [32, 64, 128], P(('grp', 'sec')), parts along dimension 0, may hold values from 0.05 to 0.8
- left_ops: bfloat16 [1024, 64, 64], P(('grp', 'sec')), parts along dimension 0, may hold values from -0.75 to 0.75
- right_ops: bfloat16 [1024, 128, 128], P(('grp', 'sec')), parts along dimension 0, may hold values from -0.0234375 to 0.0234375
- term_src: int32 [16384], P(('grp', 'sec')), parts along dimension 0, may hold values from 0 to 15
- term_tgt: int32 [16384], P(('grp', 'sec')), parts along dimension 0, may hold values from 0 to 15
- term_grp: int32 [16384], P(('grp', 'sec')), parts along dimension 0, may hold values from 0 to 31
Outputs:
- psi_final: float32 [32, 64, 128], P(('grp', 'sec')), parts along dimension 0
- sigma_final: float32 [32, 64, 128], P(('grp', 'sec')), parts along dimension 0
- rhos: float32 [6], P('grp'), parts along dimension 0
The draws below stay inside these ranges and needn't reach their ends.
There are 2 independent parts, one for each index of `grp`. The reference program is written for one: setup_inputs(seed, part) draws one part's arguments, and reference() takes and returns one part's arrays. A program takes and returns all parts, laid end to end along the dimension named above; each array names one. Nothing has to cross between parts.
Inputs may be any that keep to these rules, and one draw needn't show every extreme that they name: `term_src`: sector indices. `term_tgt`: sector indices. `term_grp`: local group indices.
All inputs are finite; a program needn't handle non-finite values.
Results may differ from the reference program's by a relative error of at most 0.0045.
Values may be sent and summed in bfloat16 or wider, within the bound.
A program may use at most 128 MiB of HBM per device.

```python
import math
import jax
import jax.numpy as jnp
import numpy as np
from jax import lax

BL = 64
BR = 128
K_DEV = 512
G_DEV = 32
ITERS = 3
SECTORS = 16
TERMS = 8192
GROUPS = 512
N_SEC = 16


def with_ends(result, key, smallest, high):
    longest = result.shape.index(max(result.shape))
    spots = []
    for shift in (0, 1):
        where = [jax.random.randint(jax.random.fold_in(key, axis), (), 0, length) for axis, length in enumerate(result.shape)]
        where[longest] = (where[longest] + shift) % result.shape[longest]
        spots.append(tuple(where))
    return result.at[spots[0]].set(smallest).at[spots[1]].set(high)


def shard_levels(rng, shape, shards, least, largest):
    level = 1.0
    for axis_at, blocks in shards:
        draws = jax.random.uniform(jax.random.fold_in(jax.random.fold_in(rng, 6), axis_at), (blocks,), jnp.float32, least / len(shards), largest / len(shards))
        level = level * jnp.repeat(jnp.exp(draws), shape[axis_at] // blocks).reshape((-1,) + (1,) * (len(shape) - 1 - axis_at))
    return level


def cumulative_ranks(number_of, skew):
    portions = [(1 << 20) // math.isqrt(standing ** skew) + 1 for standing in range(1, number_of + 1)]
    scale = 1 + sum(portions) // (1 << 30)
    return np.cumsum(np.array([max(1, weight // scale) for weight in portions]))


def ranked_ids(own_key, dims, number_of, skew):
    listing = cumulative_ranks(number_of, skew)
    lot = jax.random.randint(jax.random.fold_in(own_key, 1), dims, 0, int(listing[number_of - 1]))
    rank = jnp.searchsorted(jnp.asarray(listing, jnp.int32), lot, side="right")
    return jax.random.permutation(jax.random.fold_in(own_key, 2), number_of)[rank].astype(jnp.int32)


def scatter_about(rng, shape, deviation, reach, pieces=(), kind=jnp.bfloat16):
    result = jax.random.normal(rng, shape, jnp.float32) * deviation
    if len(pieces) > 0:
        result = shard_levels(rng, shape, pieces, -0.22, 0.18) * result
    return jnp.clip(result, min=-reach, max=reach).astype(kind)


def setup_inputs(seed: int = 0, part: int = 0) -> dict:
    arg_keys = jax.random.split(jax.random.key(seed), 8)
    part_keys = jax.random.split(jax.random.fold_in(arg_keys[7], part), 8)
    return {
        "psi_init": scatter_about(part_keys[0], (SECTORS, BL, BR), 1.0, 6.0, ((0, 16),), jnp.float32),
        "precond": jnp.clip(jnp.exp(math.log(0.8) - 2.7725887 * jax.random.uniform(part_keys[1], (SECTORS, BL, BR), jnp.float32) ** shard_levels(part_keys[1], (SECTORS, BL, BR), ((0, 16),), -0.2, 0.2)), 0.05, 0.8),
        "left_ops": scatter_about(part_keys[2], (GROUPS, BL, BL), BL ** -0.5, 0.75, ((0, 16),)),
        "right_ops": scatter_about(part_keys[3], (GROUPS, BR, BR), (BR * K_DEV) ** -0.5, 0.0234375, ((0, 16),)),
        "term_src": with_ends(jax.random.randint(part_keys[4], (TERMS,), 0, SECTORS), jax.random.fold_in(part_keys[4], 1), 0, SECTORS - 1).astype(jnp.int32),
        "term_tgt": with_ends(ranked_ids(part_keys[5], (TERMS,), SECTORS, 2), jax.random.fold_in(part_keys[5], 3), 0, SECTORS - 1).astype(jnp.int32),
        "term_grp": with_ends(jax.random.randint(part_keys[6], (TERMS,), 0, G_DEV), jax.random.fold_in(part_keys[6], 1), 0, G_DEV - 1).astype(jnp.int32),
    }


def apply_terms(psi, left_ops, right_ops, term_src, term_tgt, term_grp):
    trial = psi.astype(jnp.bfloat16)

    def one_device(carry, index):
        start = (index * K_DEV).astype(jnp.int32)
        sources = lax.dynamic_slice_in_dim(term_src, start, K_DEV)
        targets = lax.dynamic_slice_in_dim(term_tgt, start, K_DEV)
        groups = lax.dynamic_slice_in_dim(term_grp, start, K_DEV) + (index * G_DEV).astype(jnp.int32)
        lefts = left_ops[groups].astype(jnp.float32)
        rights = right_ops[groups].astype(jnp.float32)
        blocks = trial[sources].astype(jnp.float32)
        half = jnp.einsum('kab,kbc->kac', lefts, blocks).astype(jnp.bfloat16)
        parts = jnp.einsum('kac,kcd->kad', half.astype(jnp.float32), rights)
        return (carry.at[targets].add(parts), None)
    start_sigma = jnp.zeros(psi.shape, jnp.float32)
    sigma, unused = lax.scan(one_device, start_sigma, jnp.arange(N_SEC, dtype=jnp.int32))
    return sigma

def reference(psi_init, precond, left_ops, right_ops, term_src, term_tgt, term_grp):
    psi = psi_init
    quotients = []
    sigma = psi
    for step in range(ITERS):
        sigma = apply_terms(psi, left_ops, right_ops, term_src, term_tgt, term_grp)
        rho = jnp.sum(psi * sigma) / jnp.sum(psi * psi)
        quotients.append(rho)
        fresh = psi - precond * (sigma - rho * psi)
        psi = fresh / jnp.sqrt(jnp.sum(fresh * fresh) + 1e-06)
    return (psi, sigma, jnp.stack(quotients))
```

```python
import functools

import jax
import jax.numpy as jnp
from jax import lax
from jax.experimental import pallas as pl
from jax.experimental.pallas import tpu as pltpu
from jax.sharding import PartitionSpec as P

ITERS = 3
F32 = jnp.float32
BF16 = jnp.bfloat16
MESH = pl.DeviceIdType.MESH


def kernel(
    n, count, groups, bl, br, chunk,
    term_ref, psi_ref, pre_ref, left_ref, right_ref,
    psi_out, sig_out, rho_out,
    psi_recv, pre_recv, u_recv, s_recv, sib_send, sib_recv, sig_send, sig_recv, full_send, full_recv,
    own, all_psi, plan_buf, keep_buf, place_buf, src_ref, keep_ref, place_ref, plan_sem, seg, left2, a_buf, send_sem, recv_sem,
):
    me = lax.axis_index("sec")
    chips = n // 2
    core = lax.rem(me, 2)
    chip = me // 2
    sibling = me + 1 - 2 * core
    PSI, PRE, SIB, SIG, SCAL, UPD = 0, 1, 2, 2 + ITERS, 2 + 2 * ITERS, 2 + 3 * ITERS

    def push(stage, source, target, peer):
        pltpu.make_async_remote_copy(
            src_ref=source,
            dst_ref=target,
            send_sem=send_sem.at[stage],
            recv_sem=recv_sem.at[stage],
            device_id={"sec": peer},
            device_id_type=MESH,
        ).start()

    def push_all(stage, ref):
        def one(d, _):
            push(stage, ref.at[me], ref.at[me], lax.rem(me + d, n))
            return 0

        lax.fori_loop(1, n, one, 0)

    def wait_for(sem, stage, span):
        pltpu.make_async_copy(span, span, sem.at[stage]).wait()

    others = pl.ds(0, n - 1)
    other_chips = pl.ds(0, chips - 1)

    barrier = pltpu.get_barrier_semaphore()

    def greet(d, _):
        pl.semaphore_signal(barrier, inc=1, device_id={"sec": lax.rem(me + d, n)}, device_id_type=MESH)
        return 0

    lax.fori_loop(1, n, greet, 0)
    psi_recv[me] = psi_ref[0].astype(BF16)
    pre_recv[me] = pre_ref[0].astype(BF16)
    pl.semaphore_wait(barrier, n - 1)
    push_all(PSI, psi_recv)
    push_all(PRE, pre_recv)

    psi_out[0] = psi_ref[0]
    seg[count] = jnp.zeros((2 * bl, br), BF16)

    def double(g, _):
        left2[g] = jnp.concatenate([left_ref[g], left_ref[g]], axis=1)
        return 0

    lax.fori_loop(0, groups, double, 0)
    sort_terms(term_ref, plan_buf, keep_buf, place_buf, n, count, groups)
    moves = [
        pltpu.make_async_copy(a, b, plan_sem.at[i])
        for i, (a, b) in enumerate([(plan_buf, src_ref), (keep_buf, keep_ref), (place_buf, place_ref)])
    ]
    for move in moves:
        move.start()
    for move in moves:
        move.wait()
    wait_for(recv_sem, PSI, psi_recv.at[others])

    def unpack(s, _):
        all_psi[s] = psi_recv[s].astype(F32)
        return 0

    lax.fori_loop(0, n, unpack, 0)

    def apply(parity, store, split):
        depth = 2 * bl if split else bl
        lefts = left2 if split else left_ref

        def some(c, _):
            def one_group(g, _):
                first = g * n + c * (2 * chunk) + parity
                blocks = [seg[jnp.clip(place_ref[0, first + 2 * t], 0, count), :depth, :] for t in range(chunk)]
                half = jnp.dot(lefts[g], jnp.concatenate(blocks, axis=1), preferred_element_type=F32)
                half = half.astype(BF16)
                lanes = pl.ds(pl.multiple_of(g * br, br), br)
                for t in range(chunk):
                    a_buf[t * bl:(t + 1) * bl, lanes] = half[:, t * br:(t + 1) * br]
                return 0

            lax.fori_loop(0, groups, one_group, 0, unroll=8)
            store(c, jnp.dot(a_buf[...], right_ref[...], preferred_element_type=F32).reshape(chunk, bl, br))
            return 0

        lax.fori_loop(0, chips // chunk, some, 0)

    unroll = 8
    for step in range(ITERS):
        last = step == ITERS - 1

        def mix(block, acc):
            for j in range(unroll):
                k = block * unroll + j
                acc = acc * keep_ref[0, k] + all_psi[jnp.clip(src_ref[0, k], 0, n - 1)]
                high = acc.astype(BF16)
                seg[k, :bl, :] = high
                if last:
                    seg[k, bl:, :] = (acc - high.astype(F32)).astype(BF16)
            return acc

        lax.fori_loop(0, count // unroll, mix, jnp.zeros((bl, br), F32))

        def to_sibling(c, value):
            sib_send[pl.ds(c * chunk, chunk)] = value

        def to_owner(c, value):
            own[pl.ds(c * chunk, chunk)] = value

        if step > 0:
            wait_for(send_sem, SIB + step - 1, sib_send)
        apply(1 - core, to_sibling, last)
        push(SIB + step, sib_send, sib_recv.at[step], sibling)
        apply(core, to_owner, last)
        wait_for(recv_sem, SIB + step, sib_recv.at[step])

        if last:
            leaving, arriving = full_send, full_recv
        else:
            leaving, arriving = sig_send, sig_recv.at[step]
        if 0 < step < ITERS - 1:
            wait_for(send_sem, SIG + step - 1, sig_send.at[other_chips])

        def forward(d, _):
            to = lax.rem(chip + d, chips)
            leaving[to] = (own[to] + sib_recv[step, to]).astype(leaving.dtype)
            push(SIG + step, leaving.at[to], arriving.at[chip], 2 * to + core)
            return 0

        lax.fori_loop(1, chips, forward, 0)
        mine = own[chip] + sib_recv[step, chip]
        arriving[chip] = jnp.zeros((bl, br), arriving.dtype)
        wait_for(recv_sem, SIG + step, arriving.at[other_chips])
        sigma = lax.fori_loop(0, chips, lambda c, acc: acc + arriving[c].astype(F32), mine)

        psi = psi_out[0]
        pre = pre_ref[0]
        u = psi - pre * sigma
        v = pre * psi
        rows = [jnp.sum(x, axis=0, keepdims=True) for x in (psi * psi, psi * sigma, u * u, u * v, v * v)]
        s_recv[step, me] = jnp.concatenate(rows + [jnp.zeros((3, br), F32)], axis=0)
        push_all(SCAL + step, s_recv.at[step])
        if last:
            sig_out[0] = sigma
        else:
            u_recv[step, me] = u.astype(BF16)
            push_all(UPD + step, u_recv.at[step])
        wait_for(recv_sem, SCAL + step, s_recv.at[step, others])
        total = jnp.sum(jnp.sum(s_recv[step], axis=0), axis=1, keepdims=True)
        rho = total[1:2] / total[0:1]
        norm = total[2:3] + 2.0 * rho * total[3:4] + rho * rho * total[4:5]
        inv = 1.0 / jnp.sqrt(norm + 1e-06)
        rho_out[step:step + 1, :] = jnp.broadcast_to(rho, (1, br))
        psi_out[0] = (u + rho * v) * inv
        if not last:
            if step == 0:
                wait_for(recv_sem, PRE, pre_recv.at[others])
            wait_for(recv_sem, UPD + step, u_recv.at[step, others])

            def update(s, _):
                pre_s = pre_recv[s].astype(F32)
                all_psi[s] = (u_recv[step, s].astype(F32) + rho * (pre_s * all_psi[s])) * inv
                return 0

            lax.fori_loop(0, n, update, 0)

    rho_out[ITERS:, :] = jnp.zeros((8 - ITERS, br), F32)
    wait_for(send_sem, PSI, psi_recv.at[others])
    wait_for(send_sem, PRE, pre_recv.at[others])
    wait_for(send_sem, SIB + ITERS - 1, sib_send)
    wait_for(send_sem, SIG + ITERS - 2, sig_send.at[other_chips])
    wait_for(send_sem, SIG + ITERS - 1, full_send.at[other_chips])
    for step in range(ITERS):
        wait_for(send_sem, SCAL + step, s_recv.at[step, others])
        if step < ITERS - 1:
            wait_for(send_sem, UPD + step, u_recv.at[step, others])


def sort_terms(term_ref, src_buf, keep_buf, place_buf, n, count, groups):
    I32 = jnp.int32
    key = term_ref[2:3, :] * n + term_ref[1:2, :]
    rows = jnp.concatenate([key, term_ref[0:1, :], key, key, key, key, key, key], axis=0)
    columns = jnp.transpose(rows)
    key_col, src_col = columns[:, 0:1], columns[:, 1:2]
    at = lax.broadcasted_iota(I32, (1, count), 1)
    code = key * count + at
    code_col = key_col * count + lax.broadcasted_iota(I32, (count, 1), 0)

    def tally(which):
        return jnp.sum(jnp.where(which, 1, 0), axis=0, keepdims=True)

    rank = jnp.transpose(jnp.broadcast_to(tally(code_col < code), (8, count)))[:, 0:1]
    here = rank == at
    sources = jnp.sum(jnp.where(here, src_col, 0), axis=0, keepdims=True)
    src_buf[...] = jnp.clip(sources, 0, n - 1)
    ordered = jnp.sum(jnp.where(here, key_col + 1, 0), axis=0, keepdims=True)
    before = jnp.sum(jnp.where(rank + 1 == at, key_col + 1, 0), axis=0, keepdims=True)
    keep_buf[...] = jnp.where(ordered == before, 1.0, 0.0)
    for c in range(groups * n // count):
        pair = at + c * count
        upto = tally(key_col <= pair)
        place = jnp.where(upto > tally(key_col < pair), upto - 1, count)
        place_buf[:, c * count:(c + 1) * count] = jnp.clip(place, 0, count)


def body(n, psi_init, precond, left_ops, right_ops, term_src, term_tgt, term_grp):
    local, bl, br = psi_init.shape
    assert local == 1
    groups = left_ops.shape[0]
    count = term_src.shape[0]
    chunk = min(n // 2, 8)
    terms = jnp.stack([term_src, term_tgt, term_grp])
    assert groups * n % count == 0
    rights = right_ops.reshape(groups * br, br)
    vmem = pl.BlockSpec(memory_space=pltpu.VMEM)
    stages = 2 + 4 * ITERS
    psi, sigma, rhos = pl.pallas_call(
        functools.partial(kernel, n, count, groups, bl, br, chunk),
        out_shape=(
            jax.ShapeDtypeStruct((1, bl, br), F32),
            jax.ShapeDtypeStruct((1, bl, br), F32),
            jax.ShapeDtypeStruct((8, br), F32),
        ),
        in_specs=[vmem] * 5,
        out_specs=(vmem, vmem, vmem),
        scratch_shapes=[
            pltpu.VMEM((n, bl, br), BF16),
            pltpu.VMEM((n, bl, br), BF16),
            pltpu.VMEM((ITERS - 1, n, bl, br), BF16),
            pltpu.VMEM((ITERS, n, 8, br), F32),
            pltpu.VMEM((n // 2, bl, br), F32),
            pltpu.VMEM((ITERS, n // 2, bl, br), F32),
            pltpu.VMEM((n // 2, bl, br), BF16),
            pltpu.VMEM((ITERS - 1, n // 2, bl, br), BF16),
            pltpu.VMEM((n // 2, bl, br), F32),
            pltpu.VMEM((n // 2, bl, br), F32),
            pltpu.VMEM((n // 2, bl, br), F32),
            pltpu.VMEM((n, bl, br), F32),
            pltpu.VMEM((1, count), jnp.int32),
            pltpu.VMEM((1, count), F32),
            pltpu.VMEM((1, groups * n), jnp.int32),
            pltpu.SMEM((1, count), jnp.int32),
            pltpu.SMEM((1, count), F32),
            pltpu.SMEM((1, groups * n), jnp.int32),
            pltpu.SemaphoreType.DMA((3,)),
            pltpu.VMEM((count + 1, 2 * bl, br), BF16),
            pltpu.VMEM((groups, bl, 2 * bl), BF16),
            pltpu.VMEM((chunk * bl, groups * br), BF16),
            pltpu.SemaphoreType.DMA((stages,)),
            pltpu.SemaphoreType.DMA((stages,)),
        ],
        compiler_params=pltpu.CompilerParams(
            collective_id=0, has_side_effects=True, vmem_limit_bytes=56 * 1024 * 1024
        ),
    )(terms, psi_init, precond, left_ops, rights)
    return psi, sigma, rhos[:ITERS, 0]


def solution(mesh):
    return jax.shard_map(
        functools.partial(body, mesh.shape["sec"]),
        mesh=mesh,
        in_specs=(
            P(("grp", "sec"), None, None),
            P(("grp", "sec"), None, None),
            P(("grp", "sec"), None, None),
            P(("grp", "sec"), None, None),
            P(("grp", "sec")),
            P(("grp", "sec")),
            P(("grp", "sec")),
        ),
        out_specs=(P(("grp", "sec"), None, None), P(("grp", "sec"), None, None), P("grp")),
        check_vma=False,
    )
```

```python
import functools

import jax
import jax.numpy as jnp
from jax import lax
from jax.experimental import pallas as pl
from jax.experimental.pallas import tpu as pltpu
from jax.sharding import PartitionSpec as P

ITERS = 3
F32 = jnp.float32
BF16 = jnp.bfloat16
MESH = pl.DeviceIdType.MESH


def kernel(
    n, count, groups, bl, br,
    term_src, term_tgt, term_grp, psi_ref, pre_ref, left_ref, right_ref,
    psi_out, sig_out, rho_out,
    psi_recv, pre_recv, u_recv, s_recv, sib_send, sib_recv, sig_send, sig_recv, full_send, full_recv,
    own, all_psi, plan_buf, keep_buf, place_buf, src_ref, keep_ref, place_ref, plan_sem, seg, left2, a_buf, send_sem, recv_sem, near_sem,
):
    me = lax.axis_index("sec")
    chips = n // 2
    core = lax.rem(me, 2)
    chip = me // 2
    span = chips // 2
    side = chip // span
    sibling = me + 1 - 2 * core
    PSI, PRE, SIB, SIG, SCAL, UPD = 0, 1, 2, 2 + ITERS, 2 + 2 * ITERS, 2 + 3 * ITERS

    def push(stage, source, target, peer):
        pltpu.make_async_remote_copy(
            src_ref=source,
            dst_ref=target,
            send_sem=send_sem.at[stage],
            recv_sem=recv_sem.at[stage],
            device_id={"sec": peer},
            device_id_type=MESH,
        ).start()

    def push_all(stage, ref):
        def one(d, _):
            push(stage, ref.at[me], ref.at[me], lax.rem(me + d, n))
            return 0

        lax.fori_loop(1, n, one, 0)

    def wait_for(sem, stage, span):
        pltpu.make_async_copy(span, span, sem.at[stage]).wait()

    def gather(stage, row, ref):
        push(stage, ref.at[me], ref.at[me], sibling)

        def one(d, _):
            pltpu.make_async_remote_copy(
                src_ref=ref.at[me],
                dst_ref=ref.at[me],
                send_sem=send_sem.at[stage],
                recv_sem=near_sem.at[row, d],
                device_id={"sec": 2 * lax.rem(chip + d, chips) + core},
                device_id_type=MESH,
            ).start()
            return 0

        lax.fori_loop(1, chips, one, 0)

    def hand_on(stage, row, ref):
        def one(d, _):
            block = ref.at[2 * lax.rem(chip - d + chips, chips) + core]
            pltpu.make_async_copy(block, block, near_sem.at[row, d]).wait()
            push(stage, block, block, sibling)
            return 0

        lax.fori_loop(1, chips, one, 0)
        wait_for(recv_sem, stage, ref.at[pl.ds(0, chips)])

    others = pl.ds(0, n - 1)
    other_chips = pl.ds(0, chips - 1)

    barrier = pltpu.get_barrier_semaphore()

    def greet(d, _):
        pl.semaphore_signal(barrier, inc=1, device_id={"sec": lax.rem(me + d, n)}, device_id_type=MESH)
        return 0

    lax.fori_loop(1, n, greet, 0)
    psi_recv[me] = psi_ref[0].astype(BF16)
    pre_recv[me] = pre_ref[0].astype(BF16)
    pl.semaphore_wait(barrier, n - 1)
    gather(PSI, 0, psi_recv)

    psi_out[0] = psi_ref[0]
    seg[count] = jnp.zeros((2 * bl, br), BF16)

    def double(g, _):
        left2[g] = jnp.concatenate([left_ref[g], left_ref[g]], axis=1)
        return 0

    lax.fori_loop(0, groups, double, 0)
    sort_terms(term_src, term_tgt, term_grp, plan_buf, keep_buf, place_buf, n, count, groups)
    moves = [
        pltpu.make_async_copy(a, b, plan_sem.at[i])
        for i, (a, b) in enumerate([(plan_buf, src_ref), (keep_buf, keep_ref), (place_buf, place_ref)])
    ]
    for move in moves:
        move.start()
    for move in moves:
        move.wait()
    hand_on(PSI, 0, psi_recv)
    push_all(PRE, pre_recv)

    def unpack(s, _):
        all_psi[s] = psi_recv[s].astype(F32)
        return 0

    lax.fori_loop(0, n, unpack, 0)

    def apply(parity, start, length, out, split):
        chunk = min(length, 8)
        height = chunk * bl
        depth = 2 * bl if split else bl
        lefts = left2 if split else left_ref

        def some(c, _):
            def one_group(g, _):
                first = g * n + 2 * (start + c * chunk) + parity
                blocks = [seg[jnp.clip(place_ref[0, first + 2 * t], 0, count), :depth, :] for t in range(chunk)]
                half = jnp.dot(lefts[g], jnp.concatenate(blocks, axis=1), preferred_element_type=F32)
                half = half.astype(BF16)
                lanes = pl.ds(pl.multiple_of(g * br, br), br)
                for t in range(chunk):
                    a_buf[t * bl:(t + 1) * bl, lanes] = half[:, t * br:(t + 1) * br]
                return 0

            lax.fori_loop(0, groups, one_group, 0, unroll=8)
            prod = jnp.dot(a_buf[:height, :], right_ref[...], preferred_element_type=F32)
            out[pl.ds(start + c * chunk, chunk)] = prod.reshape(chunk, bl, br)
            return 0

        lax.fori_loop(0, length // chunk, some, 0)

    unroll = 8
    for step in range(ITERS):
        last = step == ITERS - 1

        def mix(block, acc):
            for j in range(unroll):
                k = block * unroll + j
                acc = acc * keep_ref[0, k] + all_psi[jnp.clip(src_ref[0, k], 0, n - 1)]
                high = acc.astype(BF16)
                seg[k, :bl, :] = high
                if last:
                    seg[k, bl:, :] = (acc - high.astype(F32)).astype(BF16)
            return acc

        lax.fori_loop(0, count // unroll, mix, jnp.zeros((bl, br), F32))

        if step > 0:
            wait_for(send_sem, SIB + step - 1, sib_send)
        apply(1 - core, 0, chips, sib_send, last)
        push(SIB + step, sib_send, sib_recv.at[step], sibling)
        if last:
            leaving, arriving = full_send, full_recv
        else:
            leaving, arriving = sig_send, sig_recv.at[step]
        if 0 < step < ITERS - 1:
            wait_for(send_sem, SIG + step - 1, sig_send.at[other_chips])

        def forward(to):
            leaving[to] = (own[to] + sib_recv[step, to]).astype(leaving.dtype)
            push(SIG + step, leaving.at[to], arriving.at[chip], 2 * to + core)

        def far(j, _):
            forward((1 - side) * span + j)
            return 0

        def near(d, _):
            forward(side * span + lax.rem(chip - side * span + d, span))
            return 0

        apply(core, (1 - side) * span, span, own, last)
        wait_for(recv_sem, SIB + step, sib_recv.at[step])
        lax.fori_loop(0, span, far, 0)
        apply(core, side * span, span, own, last)
        lax.fori_loop(1, span, near, 0)
        mine = own[chip] + sib_recv[step, chip]
        arriving[chip] = jnp.zeros((bl, br), arriving.dtype)
        wait_for(recv_sem, SIG + step, arriving.at[other_chips])
        sigma = lax.fori_loop(0, chips, lambda c, acc: acc + arriving[c].astype(F32), mine)

        psi = psi_out[0]
        pre = pre_ref[0]
        u = psi - pre * sigma
        v = pre * psi
        rows = [jnp.sum(x, axis=0, keepdims=True) for x in (psi * psi, psi * sigma, u * u, u * v, v * v)]
        s_recv[step, me] = jnp.concatenate(rows + [jnp.zeros((3, br), F32)], axis=0)
        if last:
            sig_out[0] = sigma
            push_all(SCAL + step, s_recv.at[step])
        else:
            u_recv[step, me] = u.astype(BF16)
            gather(UPD + step, 1 + step, u_recv.at[step])
            push_all(SCAL + step, s_recv.at[step])
            hand_on(UPD + step, 1 + step, u_recv.at[step])
        wait_for(recv_sem, SCAL + step, s_recv.at[step, others])
        total = jnp.sum(jnp.sum(s_recv[step], axis=0), axis=1, keepdims=True)
        rho = total[1:2] / total[0:1]
        norm = total[2:3] + 2.0 * rho * total[3:4] + rho * rho * total[4:5]
        inv = 1.0 / jnp.sqrt(norm + 1e-06)
        rho_out[step:step + 1, :] = jnp.broadcast_to(rho, (1, br))
        psi_out[0] = (u + rho * v) * inv
        if not last:
            if step == 0:
                wait_for(recv_sem, PRE, pre_recv.at[others])

            def update(s, _):
                pre_s = pre_recv[s].astype(F32)
                all_psi[s] = (u_recv[step, s].astype(F32) + rho * (pre_s * all_psi[s])) * inv
                return 0

            lax.fori_loop(0, n, update, 0, unroll=4)

    rho_out[ITERS:, :] = jnp.zeros((8 - ITERS, br), F32)
    wait_for(send_sem, PSI, psi_recv.at[others])
    wait_for(send_sem, PRE, pre_recv.at[others])
    wait_for(send_sem, SIB + ITERS - 1, sib_send)
    wait_for(send_sem, SIG + ITERS - 2, sig_send.at[other_chips])
    wait_for(send_sem, SIG + ITERS - 1, full_send.at[other_chips])
    for step in range(ITERS):
        wait_for(send_sem, SCAL + step, s_recv.at[step, others])
        if step < ITERS - 1:
            wait_for(send_sem, UPD + step, u_recv.at[step, others])


def sort_terms(term_src, term_tgt, term_grp, src_buf, keep_buf, place_buf, n, count, groups):
    I32 = jnp.int32
    key = term_grp[...] * n + term_tgt[...]
    rows = jnp.concatenate([key, term_src[...], key, key, key, key, key, key], axis=0)
    columns = jnp.transpose(rows)
    key_col, src_col = columns[:, 0:1], columns[:, 1:2]
    at = lax.broadcasted_iota(I32, (1, count), 1)
    code = key * count + at
    code_col = key_col * count + lax.broadcasted_iota(I32, (count, 1), 0)

    def tally(which):
        return jnp.sum(jnp.where(which, 1, 0), axis=0, keepdims=True)

    rank = jnp.transpose(jnp.broadcast_to(tally(code_col < code), (8, count)))[:, 0:1]
    here = rank == at
    sources = jnp.sum(jnp.where(here, src_col, 0), axis=0, keepdims=True)
    src_buf[...] = jnp.clip(sources, 0, n - 1)
    ordered = jnp.sum(jnp.where(here, key_col + 1, 0), axis=0, keepdims=True)
    before = jnp.sum(jnp.where(rank + 1 == at, key_col + 1, 0), axis=0, keepdims=True)
    keep_buf[...] = jnp.where(ordered == before, 1.0, 0.0)
    for c in range(groups * n // count):
        pair = at + c * count
        upto = tally(key_col <= pair)
        place = jnp.where(upto > tally(key_col < pair), upto - 1, count)
        place_buf[:, c * count:(c + 1) * count] = jnp.clip(place, 0, count)


def body(n, psi_init, precond, left_ops, right_ops, term_src, term_tgt, term_grp):
    local, bl, br = psi_init.shape
    assert local == 1
    groups = left_ops.shape[0]
    count = term_src.shape[0]
    chunk = min(n // 2, 8)
    assert groups * n % count == 0
    rights = right_ops.reshape(groups * br, br)
    vmem = pl.BlockSpec(memory_space=pltpu.VMEM)
    stages = 2 + 4 * ITERS
    psi, sigma, rhos = pl.pallas_call(
        functools.partial(kernel, n, count, groups, bl, br),
        out_shape=(
            jax.ShapeDtypeStruct((1, bl, br), F32),
            jax.ShapeDtypeStruct((1, bl, br), F32),
            jax.ShapeDtypeStruct((8, br), F32),
        ),
        in_specs=[vmem] * 7,
        out_specs=(vmem, vmem, vmem),
        scratch_shapes=[
            pltpu.VMEM((n, bl, br), BF16),
            pltpu.VMEM((n, bl, br), BF16),
            pltpu.VMEM((ITERS - 1, n, bl, br), BF16),
            pltpu.VMEM((ITERS, n, 8, br), F32),
            pltpu.VMEM((n // 2, bl, br), F32),
            pltpu.VMEM((ITERS, n // 2, bl, br), F32),
            pltpu.VMEM((n // 2, bl, br), BF16),
            pltpu.VMEM((ITERS - 1, n // 2, bl, br), BF16),
            pltpu.VMEM((n // 2, bl, br), F32),
            pltpu.VMEM((n // 2, bl, br), F32),
            pltpu.VMEM((n // 2, bl, br), F32),
            pltpu.VMEM((n, bl, br), F32),
            pltpu.VMEM((1, count), jnp.int32),
            pltpu.VMEM((1, count), F32),
            pltpu.VMEM((1, groups * n), jnp.int32),
            pltpu.SMEM((1, count), jnp.int32),
            pltpu.SMEM((1, count), F32),
            pltpu.SMEM((1, groups * n), jnp.int32),
            pltpu.SemaphoreType.DMA((3,)),
            pltpu.VMEM((count + 1, 2 * bl, br), BF16),
            pltpu.VMEM((groups, bl, 2 * bl), BF16),
            pltpu.VMEM((chunk * bl, groups * br), BF16),
            pltpu.SemaphoreType.DMA((stages,)),
            pltpu.SemaphoreType.DMA((stages,)),
            pltpu.SemaphoreType.DMA((ITERS, n // 2)),
        ],
        compiler_params=pltpu.CompilerParams(
            collective_id=0, has_side_effects=True, vmem_limit_bytes=56 * 1024 * 1024
        ),
    )(*[t.reshape(1, count) for t in (term_src, term_tgt, term_grp)], psi_init, precond, left_ops, rights)
    return psi, sigma, rhos[:ITERS, 0]


def solution(mesh):
    return jax.shard_map(
        functools.partial(body, mesh.shape["sec"]),
        mesh=mesh,
        in_specs=(
            P(("grp", "sec"), None, None),
            P(("grp", "sec"), None, None),
            P(("grp", "sec"), None, None),
            P(("grp", "sec"), None, None),
            P(("grp", "sec")),
            P(("grp", "sec")),
            P(("grp", "sec")),
        ),
        out_specs=(P(("grp", "sec"), None, None), P(("grp", "sec"), None, None), P("grp")),
        check_vma=False,
    )
```

```python
import functools

import jax
import jax.numpy as jnp
from jax import lax
from jax.experimental import pallas as pl
from jax.experimental.pallas import tpu as pltpu
from jax.sharding import PartitionSpec as P

ITERS = 3
F32 = jnp.float32
BF16 = jnp.bfloat16
MESH = pl.DeviceIdType.MESH


def kernel(
    n, count, groups, bl, br,
    term_src, term_tgt, term_grp, psi_ref, pre_ref, left_ref, right_ref,
    psi_out, sig_out, rho_out,
    psi_recv, pre_recv, u_recv, s_recv, sib_send, sib_recv, sig_send, sig_recv, full_send, full_recv,
    own, all_psi, plan_buf, keep_buf, place_buf, src_ref, keep_ref, place_ref, plan_sem, seg, left2, a_buf, send_sem, recv_sem, near_sem,
):
    me = lax.axis_index("sec")
    chips = n // 2
    core = lax.rem(me, 2)
    chip = me // 2
    span = chips // 2
    side = chip // span
    sibling = me + 1 - 2 * core
    PSI, PRE, SIB, SIG, SCAL, UPD = 0, 1, 2, 2 + ITERS, 2 + 2 * ITERS, 2 + 3 * ITERS

    def push(stage, source, target, peer):
        pltpu.make_async_remote_copy(
            src_ref=source,
            dst_ref=target,
            send_sem=send_sem.at[stage],
            recv_sem=recv_sem.at[stage],
            device_id={"sec": peer},
            device_id_type=MESH,
        ).start()

    def push_all(stage, ref):
        def one(d, _):
            push(stage, ref.at[me], ref.at[me], lax.rem(me + d, n))
            return 0

        lax.fori_loop(1, n, one, 0)

    def wait_for(sem, stage, span):
        pltpu.make_async_copy(span, span, sem.at[stage]).wait()

    def gather(stage, row, ref):
        push(stage, ref.at[me], ref.at[me], sibling)

        def one(d, _):
            pltpu.make_async_remote_copy(
                src_ref=ref.at[me],
                dst_ref=ref.at[me],
                send_sem=send_sem.at[stage],
                recv_sem=near_sem.at[row, d],
                device_id={"sec": 2 * lax.rem(chip + d, chips) + core},
                device_id_type=MESH,
            ).start()
            return 0

        lax.fori_loop(1, chips, one, 0)

    def hand_on(stage, row, ref):
        def one(d, _):
            block = ref.at[2 * lax.rem(chip - d + chips, chips) + core]
            pltpu.make_async_copy(block, block, near_sem.at[row, d]).wait()
            push(stage, block, block, sibling)
            return 0

        lax.fori_loop(1, chips, one, 0)
        wait_for(recv_sem, stage, ref.at[pl.ds(0, chips)])

    others = pl.ds(0, n - 1)
    other_chips = pl.ds(0, chips - 1)

    barrier = pltpu.get_barrier_semaphore()

    def greet(d, _):
        pl.semaphore_signal(barrier, inc=1, device_id={"sec": lax.rem(me + d, n)}, device_id_type=MESH)
        return 0

    lax.fori_loop(1, n, greet, 0)
    psi_recv[me] = psi_ref[0].astype(BF16)
    pre_recv[me] = pre_ref[0].astype(BF16)
    pl.semaphore_wait(barrier, n - 1)
    gather(PSI, 0, psi_recv)

    psi_out[0] = psi_ref[0]
    seg[count] = jnp.zeros((2 * bl, br), BF16)

    def double(g, _):
        left2[g] = jnp.concatenate([left_ref[g], left_ref[g]], axis=1)
        return 0

    lax.fori_loop(0, groups, double, 0)
    sort_terms(term_src, term_tgt, term_grp, plan_buf, keep_buf, place_buf, n, count, groups)
    moves = [
        pltpu.make_async_copy(a, b, plan_sem.at[i])
        for i, (a, b) in enumerate([(plan_buf, src_ref), (keep_buf, keep_ref), (place_buf, place_ref)])
    ]
    for move in moves:
        move.start()
    for move in moves:
        move.wait()
    hand_on(PSI, 0, psi_recv)
    push_all(PRE, pre_recv)

    def unpack(s, _):
        all_psi[s] = psi_recv[s].astype(F32)
        return 0

    lax.fori_loop(0, n, unpack, 0, unroll=4)

    def apply(parity, start, length, out, split):
        chunk = min(length, 8)
        height = chunk * bl
        depth = 2 * bl if split else bl
        lefts = left2 if split else left_ref

        def some(c, _):
            def one_group(g, _):
                first = g * n + 2 * (start + c * chunk) + parity
                blocks = [seg[jnp.clip(place_ref[0, first + 2 * t], 0, count), :depth, :] for t in range(chunk)]
                half = jnp.dot(lefts[g], jnp.concatenate(blocks, axis=1), preferred_element_type=F32)
                half = half.astype(BF16)
                lanes = pl.ds(pl.multiple_of(g * br, br), br)
                for t in range(chunk):
                    a_buf[t * bl:(t + 1) * bl, lanes] = half[:, t * br:(t + 1) * br]
                return 0

            lax.fori_loop(0, groups, one_group, 0, unroll=8)
            prod = jnp.dot(a_buf[:height, :], right_ref[...], preferred_element_type=F32)
            out[pl.ds(start + c * chunk, chunk)] = prod.reshape(chunk, bl, br)
            return 0

        lax.fori_loop(0, length // chunk, some, 0)

    unroll = 16
    for step in range(ITERS):
        last = step == ITERS - 1

        def mix(block, acc):
            for j in range(unroll):
                k = block * unroll + j
                acc = acc * keep_ref[0, k] + all_psi[jnp.clip(src_ref[0, k], 0, n - 1)]
                high = acc.astype(BF16)
                seg[k, :bl, :] = high
                if last:
                    seg[k, bl:, :] = (acc - high.astype(F32)).astype(BF16)
            return acc

        lax.fori_loop(0, count // unroll, mix, jnp.zeros((bl, br), F32))

        if step > 0:
            wait_for(send_sem, SIB + step - 1, sib_send)
        apply(1 - core, 0, chips, sib_send, last)
        push(SIB + step, sib_send, sib_recv.at[step], sibling)
        if last:
            leaving, arriving = full_send, full_recv
        else:
            leaving, arriving = sig_send, sig_recv.at[step]
        if 0 < step < ITERS - 1:
            wait_for(send_sem, SIG + step - 1, sig_send.at[other_chips])

        def forward(to):
            leaving[to] = (own[to] + sib_recv[step, to]).astype(leaving.dtype)
            push(SIG + step, leaving.at[to], arriving.at[chip], 2 * to + core)

        def far(j, _):
            forward((1 - side) * span + j)
            return 0

        def near(d, _):
            forward(side * span + lax.rem(chip - side * span + d, span))
            return 0

        apply(core, (1 - side) * span, span, own, last)
        wait_for(recv_sem, SIB + step, sib_recv.at[step])
        lax.fori_loop(0, span, far, 0)
        apply(core, side * span, span, own, last)
        lax.fori_loop(1, span, near, 0)
        mine = own[chip] + sib_recv[step, chip]
        arriving[chip] = jnp.zeros((bl, br), arriving.dtype)
        wait_for(recv_sem, SIG + step, arriving.at[other_chips])
        sigma = lax.fori_loop(0, chips, lambda c, acc: acc + arriving[c].astype(F32), mine)

        psi = psi_out[0]
        pre = pre_ref[0]
        u = psi - pre * sigma
        v = pre * psi
        if not last:
            u_recv[step, me] = u.astype(BF16)
            gather(UPD + step, 1 + step, u_recv.at[step])
        rows = [jnp.sum(x, axis=0, keepdims=True) for x in (psi * psi, psi * sigma, u * u, u * v, v * v)]
        s_recv[step, me] = jnp.concatenate(rows + [jnp.zeros((3, br), F32)], axis=0)
        if last:
            sig_out[0] = sigma
            push_all(SCAL + step, s_recv.at[step])
        else:
            push_all(SCAL + step, s_recv.at[step])
            hand_on(UPD + step, 1 + step, u_recv.at[step])
        wait_for(recv_sem, SCAL + step, s_recv.at[step, others])
        total = jnp.sum(jnp.sum(s_recv[step], axis=0), axis=1, keepdims=True)
        rho = total[1:2] / total[0:1]
        norm = total[2:3] + 2.0 * rho * total[3:4] + rho * rho * total[4:5]
        inv = 1.0 / jnp.sqrt(norm + 1e-06)
        rho_out[step:step + 1, :] = jnp.broadcast_to(rho, (1, br))
        psi_out[0] = (u + rho * v) * inv
        if not last:
            if step == 0:
                wait_for(recv_sem, PRE, pre_recv.at[others])

            def update(s, _):
                pre_s = pre_recv[s].astype(F32)
                all_psi[s] = (u_recv[step, s].astype(F32) + rho * (pre_s * all_psi[s])) * inv
                return 0

            lax.fori_loop(0, n, update, 0, unroll=4)

    rho_out[ITERS:, :] = jnp.zeros((8 - ITERS, br), F32)
    wait_for(send_sem, PSI, psi_recv.at[others])
    wait_for(send_sem, PRE, pre_recv.at[others])
    wait_for(send_sem, SIB + ITERS - 1, sib_send)
    wait_for(send_sem, SIG + ITERS - 2, sig_send.at[other_chips])
    wait_for(send_sem, SIG + ITERS - 1, full_send.at[other_chips])
    for step in range(ITERS):
        wait_for(send_sem, SCAL + step, s_recv.at[step, others])
        if step < ITERS - 1:
            wait_for(send_sem, UPD + step, u_recv.at[step, others])


def sort_terms(term_src, term_tgt, term_grp, src_buf, keep_buf, place_buf, n, count, groups):
    I32 = jnp.int32
    key = term_grp[...] * n + term_tgt[...]
    rows = jnp.concatenate([key, term_src[...], key, key, key, key, key, key], axis=0)
    columns = jnp.transpose(rows)
    key_col, src_col = columns[:, 0:1], columns[:, 1:2]
    at = lax.broadcasted_iota(I32, (1, count), 1)
    code = key * count + at
    code_col = key_col * count + lax.broadcasted_iota(I32, (count, 1), 0)

    def tally(which):
        return jnp.sum(jnp.where(which, 1, 0), axis=0, keepdims=True)

    rank = jnp.transpose(jnp.broadcast_to(tally(code_col < code), (8, count)))[:, 0:1]
    here = rank == at
    sources = jnp.sum(jnp.where(here, src_col, 0), axis=0, keepdims=True)
    src_buf[...] = jnp.clip(sources, 0, n - 1)
    ordered = jnp.sum(jnp.where(here, key_col + 1, 0), axis=0, keepdims=True)
    before = jnp.sum(jnp.where(rank + 1 == at, key_col + 1, 0), axis=0, keepdims=True)
    keep_buf[...] = jnp.where(ordered == before, 1.0, 0.0)
    for c in range(groups * n // count):
        pair = at + c * count
        upto = tally(key_col <= pair)
        place = jnp.where(upto > tally(key_col < pair), upto - 1, count)
        place_buf[:, c * count:(c + 1) * count] = jnp.clip(place, 0, count)


def body(n, psi_init, precond, left_ops, right_ops, term_src, term_tgt, term_grp):
    local, bl, br = psi_init.shape
    assert local == 1
    groups = left_ops.shape[0]
    count = term_src.shape[0]
    chunk = min(n // 2, 8)
    assert groups * n % count == 0
    rights = right_ops.reshape(groups * br, br)
    vmem = pl.BlockSpec(memory_space=pltpu.VMEM)
    stages = 2 + 4 * ITERS
    psi, sigma, rhos = pl.pallas_call(
        functools.partial(kernel, n, count, groups, bl, br),
        out_shape=(
            jax.ShapeDtypeStruct((1, bl, br), F32),
            jax.ShapeDtypeStruct((1, bl, br), F32),
            jax.ShapeDtypeStruct((8, br), F32),
        ),
        in_specs=[vmem] * 7,
        out_specs=(vmem, vmem, vmem),
        scratch_shapes=[
            pltpu.VMEM((n, bl, br), BF16),
            pltpu.VMEM((n, bl, br), BF16),
            pltpu.VMEM((ITERS - 1, n, bl, br), BF16),
            pltpu.VMEM((ITERS, n, 8, br), F32),
            pltpu.VMEM((n // 2, bl, br), F32),
            pltpu.VMEM((ITERS, n // 2, bl, br), F32),
            pltpu.VMEM((n // 2, bl, br), BF16),
            pltpu.VMEM((ITERS - 1, n // 2, bl, br), BF16),
            pltpu.VMEM((n // 2, bl, br), F32),
            pltpu.VMEM((n // 2, bl, br), F32),
            pltpu.VMEM((n // 2, bl, br), F32),
            pltpu.VMEM((n, bl, br), F32),
            pltpu.VMEM((1, count), jnp.int32),
            pltpu.VMEM((1, count), F32),
            pltpu.VMEM((1, groups * n), jnp.int32),
            pltpu.SMEM((1, count), jnp.int32),
            pltpu.SMEM((1, count), F32),
            pltpu.SMEM((1, groups * n), jnp.int32),
            pltpu.SemaphoreType.DMA((3,)),
            pltpu.VMEM((count + 1, 2 * bl, br), BF16),
            pltpu.VMEM((groups, bl, 2 * bl), BF16),
            pltpu.VMEM((chunk * bl, groups * br), BF16),
            pltpu.SemaphoreType.DMA((stages,)),
            pltpu.SemaphoreType.DMA((stages,)),
            pltpu.SemaphoreType.DMA((ITERS, n // 2)),
        ],
        compiler_params=pltpu.CompilerParams(
            collective_id=0, has_side_effects=True, vmem_limit_bytes=56 * 1024 * 1024
        ),
    )(*[t.reshape(1, count) for t in (term_src, term_tgt, term_grp)], psi_init, precond, left_ops, rights)
    return psi, sigma, rhos[:ITERS, 0]


def solution(mesh):
    return jax.shard_map(
        functools.partial(body, mesh.shape["sec"]),
        mesh=mesh,
        in_specs=(
            P(("grp", "sec"), None, None),
            P(("grp", "sec"), None, None),
            P(("grp", "sec"), None, None),
            P(("grp", "sec"), None, None),
            P(("grp", "sec")),
            P(("grp", "sec")),
            P(("grp", "sec")),
        ),
        out_specs=(P(("grp", "sec"), None, None), P(("grp", "sec"), None, None), P("grp")),
        check_vma=False,
    )
```
